32 devices in a mesh: gx: 4 (over z), gy: 4 (over x, core), gz: 2 (over y).
Axes of the slice: x: 2, y: 2, z: 4, core: 2. Of those that a mesh axis runs over, the one named last changes fastest.
Arguments:
- composition: float32 [106, 8, 16, 256], P(None, 'gx', 'gy', 'gz'), may hold values from -6 to 6
- inv_temp: bfloat16 [8, 16, 256], P('gx', 'gy', 'gz'), may hold values from 0.3984375 to 1.59375
- diffusivity: float32 [106], replicated, may hold values from 0.01 to 0.1
- reactant_orders: bfloat16 [420, 106], replicated, may hold values from 0 to 0.019897461
- net_stoich: bfloat16 [106, 420], replicated, may hold values from -0.3125 to 0.3125
- log_rate: float32 [420], replicated, may hold values from -1 to 1
- activation: float32 [420], replicated, may hold values from 0.5 to 3
- hot_blocks: int32 [4, 4, 2, 8], P('gx', 'gy', 'gz'), may hold values from 0 to 7, as said below
- hot_counts: int32 [4, 4, 2], P('gx', 'gy', 'gz'), may hold values from 1 to 8, as said below
Outputs:
- composition_next: float32 [106, 8, 16, 256], P(None, 'gx', 'gy', 'gz')
The draws below stay inside these ranges and needn't reach their ends.
Inputs may be any that keep to these rules, and one draw needn't show every extreme that they name: `hot_blocks`: each device's row holds 8 distinct block numbers of that device. `hot_counts`: some device has exactly 8 hot blocks.
All inputs are finite; a program needn't handle non-finite values.
Results may differ from the reference program's by a relative error of at most 0.0015.
Values may be sent and summed in bfloat16 or wider, within the bound.
A program may use at most 64 MiB of HBM per device.

```python
import math
import jax
import jax.numpy as jnp
from jax import lax

S = 106
R = 420
CZ = 128
SECTIONS = 4
CX = 2
CY = 4
HOT = 8
NX = 8
NY = 16
NZ = 256
N_GX = 4
N_GY = 4
N_GZ = 2
DEVICES = 32


def draw_hot_blocks(key, part):
    keys = jax.random.split(jax.random.fold_in(key, 11), DEVICES)

    def choose_row(row_key):
        return jax.random.permutation(row_key, CX * CY)[:HOT]
    rows = jax.vmap(choose_row)(keys)
    return rows.astype(jnp.int32).reshape(N_GX, N_GY, N_GZ, HOT)


def draw_hot_counts(key, part):
    folded = jax.random.fold_in(key, 23)
    drawn = jax.random.randint(folded, (DEVICES,), 0, HOT)
    counts = 1 + drawn * drawn // HOT
    picked = jax.random.randint(jax.random.fold_in(folded, 1), (), 0, DEVICES)
    counts = jnp.where(jnp.arange(DEVICES) == picked, HOT, counts)
    counts = jnp.minimum(counts, HOT)
    return counts.astype(jnp.int32).reshape(N_GX, N_GY, N_GZ)


def shard_levels(stream_key, dims, cuts, smallest, high):
    loudness = 1.0
    for dim, shards_of in cuts:
        heights = jax.random.uniform(jax.random.fold_in(jax.random.fold_in(stream_key, 6), dim), (shards_of,), jnp.float32, smallest / len(cuts), high / len(cuts))
        loudness = loudness * jnp.repeat(jnp.exp(heights), dims[dim] // shards_of).reshape((-1,) + (1,) * (len(dims) - 1 - dim))
    return loudness


def bell_draw(key, shape, width, bound, shards=(), kind=jnp.bfloat16):
    values = jax.random.normal(key, shape, jnp.float32) * width
    if len(shards) > 0:
        values = shard_levels(key, shape, shards, -0.22, 0.18) * values
    return jnp.clip(values, min=-bound, max=bound).astype(kind)


def setup_inputs(seed: int = 0) -> dict:
    splits = jax.random.split(jax.random.key(seed), 10)
    return {
        "composition": bell_draw(splits[0], (S, NX, NY, NZ), 1.0, 6.0, ((1, 4), (2, 4), (3, 2)), jnp.float32),
        "inv_temp": jnp.clip(jnp.exp(math.log(1.59375) - 1.3862944 * jax.random.uniform(splits[1], (NX, NY, NZ), jnp.float32) ** shard_levels(splits[1], (NX, NY, NZ), ((0, 4), (1, 4), (2, 2)), -0.2, 0.2)), 0.3984375, 1.59375).astype(jnp.bfloat16),
        "diffusivity": jnp.clip(jnp.exp(jax.random.uniform(splits[2], (S,), jnp.float32, math.log(0.01), math.log(0.1))), 0.01, 0.1),
        "reactant_orders": jnp.clip(jax.random.uniform(splits[3], (R, S), jnp.float32, 0.0, 0.019897461), 0.0, 0.019897461).astype(jnp.bfloat16),
        "net_stoich": bell_draw(splits[4], (S, R), R ** -0.5, 0.3125),
        "log_rate": jnp.clip(jax.random.uniform(splits[5], (R,), jnp.float32, -1.0, 1.0), -1.0, 1.0),
        "activation": jnp.clip(jax.random.uniform(splits[6], (R,), jnp.float32, 0.5, 3.0), 0.5, 3.0),
        "hot_blocks": draw_hot_blocks(jax.random.fold_in(splits[9], 71), 0),
        "hot_counts": draw_hot_counts(jax.random.fold_in(splits[9], 71), 0),
    }


rate_step = 0.5


def fourth_order(padded, axis_number, length):
    def window(offset):
        return lax.slice_in_dim(padded, offset, offset + length, axis=axis_number)
    return (16.0 * (window(1) + window(3)) - window(0) - window(4) - 30.0 * window(2)) / 12.0


def transport(field_in, diffusivity):
    field_shape = field_in.shape
    padded = jnp.pad(field_in, ((0, 0), (2, 2), (2, 2), (2, 2)), mode="wrap")
    along_x = padded[:, :, 2:-2, 2:-2]
    along_y = padded[:, 2:-2, :, 2:-2]
    along_z = padded[:, 2:-2, 2:-2, :]
    laplace_sum = fourth_order(along_x, 1, field_shape[1]) + fourth_order(along_y, 2, field_shape[2]) + fourth_order(along_z, 3, field_shape[3])
    return field_in + diffusivity[:, None, None, None] * laplace_sum


def react_cells(columns, inverse, reactant_orders, net_stoich, log_rate, activation):
    initial = columns.astype(jnp.float32)
    current = initial
    operand = columns
    inverse_cells = inverse.astype(jnp.float32)
    for repeat in range(SECTIONS):
        logits = jnp.dot(reactant_orders, operand, preferred_element_type=jnp.float32) + log_rate[:, None] - activation[:, None] * inverse_cells[None, :]
        progress = jnp.exp(logits).astype(jnp.bfloat16)
        produced = jnp.dot(net_stoich, progress, preferred_element_type=jnp.float32)
        consumed = lax.dot_general(reactant_orders, progress, (((0,), (0,)), ((), ())), preferred_element_type=jnp.float32)
        current = current + rate_step * produced / (1.0 + rate_step * consumed)
        operand = current.astype(jnp.bfloat16)
    return (current - initial).astype(jnp.bfloat16)


def reference(composition, inv_temp, diffusivity, reactant_orders, net_stoich, log_rate, activation, hot_blocks, hot_counts):
    carried = transport(composition, diffusivity)
    device_count = N_GX * N_GY * N_GZ
    blocks_total = CX * CY
    shaped = carried.reshape(S, N_GX, CX, N_GY, CY, N_GZ, CZ).transpose(1, 3, 5, 0, 2, 4, 6).reshape(device_count, S, blocks_total, CZ)
    heat_rows = inv_temp.reshape(N_GX, CX, N_GY, CY, N_GZ, CZ).transpose(0, 2, 4, 1, 3, 5).reshape(device_count, blocks_total, CZ)
    listed_all = hot_blocks.reshape(device_count, HOT)
    counts = hot_counts.reshape(device_count)

    def one_device(packed):
        state_field, heat_block, listed, live_count = packed

        def advance(slot, state_field):
            block_index = listed[slot].astype(jnp.int32)
            column_block = lax.dynamic_slice_in_dim(state_field, block_index, 1, 1).reshape(S, CZ)
            inverse = lax.dynamic_slice_in_dim(heat_block, block_index, 1, 0).reshape(CZ)
            increment = react_cells(column_block.astype(jnp.bfloat16), inverse, reactant_orders, net_stoich, log_rate, activation)
            updated = (column_block + increment.astype(jnp.float32)).reshape(S, 1, CZ)
            return lax.dynamic_update_slice_in_dim(state_field, updated, block_index, 1)

        return lax.fori_loop(jnp.int32(0), live_count.astype(jnp.int32), advance, state_field)

    reacted = lax.map(one_device, (shaped, heat_rows, listed_all, counts))
    returned = reacted.reshape(N_GX, N_GY, N_GZ, S, CX, CY, CZ).transpose(3, 0, 4, 1, 5, 2, 6).reshape(S, N_GX * CX, N_GY * CY, N_GZ * CZ)
    return transport(returned, diffusivity)
```

```python
import functools

import jax
import jax.numpy as jnp
from jax import lax
from jax.experimental import pallas as pl
from jax.experimental.pallas import tpu as pltpu
from jax.sharding import PartitionSpec as P

SECTIONS = 4
MESH = pl.DeviceIdType.MESH
F32, BF16 = jnp.float32, jnp.bfloat16
GROUP = 1


def up(value, step):
    return (value + step - 1) // step * step


def kernel(
    cells_x, cells_y, species, reactions,
    comp_ref, inv_ref, diff_ref, orders_ref, net_ref, rate_ref, act_ref, blocks_ref, counts_ref,
    out_ref,
    field, send, edges_out, from_low_x, from_high_x, from_low_y, from_high_y, edges_low, edges_high,
    orders_pad, orders_t, logit_w, gain_w,
    sems_x, sems_y, sems_z,
):
    size_x, size_y, size_z = (lax.axis_size(a) for a in ("gx", "gy", "gz"))
    rows = field.shape[3]
    lanes = field.shape[4]
    blocks = cells_x * cells_y

    def beside(axis, size, step):
        return {axis: lax.rem(lax.axis_index(axis) + (step + size), size)}

    low_x, high_x = beside("gx", size_x, -1), beside("gx", size_x, 1)
    low_y, high_y = beside("gy", size_y, -1), beside("gy", size_y, 1)
    low_z, high_z = beside("gz", size_z, -1), beside("gz", size_z, 1)
    others = [low_x, high_x, low_y, high_y, high_z] + ([low_z] if size_z > 2 else [])

    barrier = pltpu.get_barrier_semaphore()
    for other in others:
        pl.semaphore_signal(barrier, inc=1, device_id=other, device_id_type=MESH)

    lane = lax.broadcasted_iota(jnp.int32, (rows, lanes), 1)
    edge = (lane < 2) | (lane >= lanes - 2)
    place = lane % 4

    def number(x, y):
        return x * cells_y + y

    def copy(src, dst, sems, index, target):
        return pltpu.make_async_remote_copy(
            src_ref=src, dst_ref=dst, send_sem=sems.at[0, index], recv_sem=sems.at[1, index],
            device_id=target, device_id_type=MESH,
        )

    def x_copies(stage, y):
        base = (stage * cells_y + y) * 2
        return [
            copy(send.at[stage, y, pl.ds(cells_x - 2, 2)], from_low_x.at[stage, y], sems_x, base, high_x),
            copy(send.at[stage, y, pl.ds(0, 2)], from_high_x.at[stage, y], sems_x, base + 1, low_x),
        ]

    def y_copies(stage):
        made = {}
        for k in range(2):
            base = (stage * 2 + k) * 2
            made.setdefault(cells_y - 2 + k, []).append(
                copy(send.at[stage, cells_y - 2 + k], from_low_y.at[stage, k], sems_y, base, high_y)
            )
            made.setdefault(k, []).append(
                copy(send.at[stage, k], from_high_y.at[stage, k], sems_y, base + 1, low_y)
            )
        return made

    def y_low(stage, k):
        return copy(send.at[stage, cells_y - 2 + k], from_low_y.at[stage, k], sems_y, (stage * 2 + k) * 2, high_y)

    def y_high(stage, k):
        return copy(send.at[stage, k], from_high_y.at[stage, k], sems_y, (stage * 2 + k) * 2 + 1, low_y)

    def z_copies(stage):
        made = [copy(edges_out.at[stage], edges_low.at[stage], sems_z, stage * 2, high_z)]
        if size_z > 2:
            made.append(copy(edges_out.at[stage], edges_high.at[stage], sems_z, stage * 2 + 1, low_z))
        return made

    def pack(value, index):
        return pltpu.roll(value, (4 * index + 2) % lanes, 1)

    def edge_terms(stage, own):
        low = edges_low[stage].astype(F32)
        got = low if size_z == 2 else jnp.where(place >= 2, edges_high[stage].astype(F32), low)
        d = got - own
        far = jnp.where(place < 2, pltpu.roll(d, lanes - 2, 1), pltpu.roll(d, 2, 1))
        near = jnp.where(place == 1, pltpu.roll(d, lanes - 1, 1), pltpu.roll(d, 1, 1))
        return jnp.where((place == 1) | (place == 2), 16.0 * near, 0.0) - far

    def at_x(stage, x, y):
        if x < 0:
            return from_low_x[stage, y, 2 + x].astype(F32)
        if x >= cells_x:
            return from_high_x[stage, y, x - cells_x].astype(F32)
        return field[stage, y, x]

    def at_y(stage, x, y):
        if y < 0:
            return from_low_y[stage, 2 + y, x].astype(F32)
        if y >= cells_y:
            return from_high_y[stage, y - cells_y, x].astype(F32)
        return field[stage, y, x]

    def diffuse(stage, x, y, scale, terms):
        v = field[stage, y, x]
        near = (
            at_x(stage, x - 1, y) + at_x(stage, x + 1, y) + at_y(stage, x, y - 1) + at_y(stage, x, y + 1)
            + pltpu.roll(v, 1, 1) + pltpu.roll(v, lanes - 1, 1)
        )
        far = (
            at_x(stage, x - 2, y) + at_x(stage, x + 2, y) + at_y(stage, x, y - 2) + at_y(stage, x, y + 2)
            + pltpu.roll(v, 2, 1) + pltpu.roll(v, lanes - 2, 1)
        )
        index = number(x, y)
        fix = jnp.where(edge, pltpu.roll(terms, (2 * lanes - 4 * index - 2) % lanes, 1), 0.0)
        return v + scale * (16.0 * near - far - 90.0 * v + fix)

    packed = jnp.zeros((rows, lanes), F32)
    for y in range(cells_y):
        for x in range(cells_x):
            field[0, y, x, pl.ds(species // 8 * 8, rows - species // 8 * 8), :] = jnp.zeros(
                (rows - species // 8 * 8, lanes), F32
            )
            field[0, y, x, pl.ds(0, species), :] = comp_ref[pl.ds(number(x, y), species, stride=blocks), :]
            v = field[0, y, x]
            send[0, y, x] = v.astype(BF16)
            packed = jnp.where(lane // 4 == number(x, y), pack(v, number(x, y)), packed)
    edges_out[0] = packed.astype(BF16)

    pl.semaphore_wait(barrier, len(others))
    waits_send = []

    def start(copies):
        for c in copies:
            c.start()
            waits_send.append(c)

    first_x = [x_copies(0, y) for y in range(cells_y)]
    first_y = y_copies(0)
    first_z = z_copies(0)
    start(first_z)
    for y in range(cells_y):
        start(first_x[y])
        start(first_y.get(y, []))

    wide = orders_t.shape[1]
    orders_pad[...] = jnp.zeros_like(orders_pad)
    orders_pad[pl.ds(0, reactions), pl.ds(0, species)] = orders_ref[...].astype(F32)
    transposed = orders_pad[...].T
    used = logit_w.shape[0]
    gain_w[...] = jnp.zeros_like(gain_w)
    gain_w[pl.ds(0, species), pl.ds(0, reactions)] = (0.5 * net_ref[...].astype(F32)).astype(BF16)
    gain_w[pl.ds(rows, rows), :] = (0.5 * transposed[:rows, :used]).astype(BF16)
    orders_t[...] = transposed
    for k, (ref, sign) in enumerate(((rate_ref, 1.0), (act_ref, -1.0))):
        value = sign * ref[...]
        upper = value.astype(BF16).astype(F32)
        orders_t[pl.ds(species + 2 * k, 1), pl.ds(0, reactions)] = upper
        orders_t[pl.ds(species + 2 * k + 1, 1), pl.ds(0, reactions)] = value - upper
    logit_w[...] = orders_t[...].T[:used, :rows].astype(BF16)
    number_row = diff_ref[...] * (1.0 / 12.0)
    orders_pad[pl.ds(0, lanes), :] = jnp.zeros((lanes, orders_pad.shape[1]), F32)
    orders_pad[pl.ds(0, lanes), pl.ds(0, species)] = jnp.broadcast_to(number_row, (lanes, species))
    scale = orders_pad[pl.ds(0, lanes), :].T[:rows, :]

    inverse = inv_ref[...].astype(F32)
    count = counts_ref[0]
    hot = []
    for index in range(blocks):
        found = jnp.int32(0)
        for k in range(blocks_ref.shape[0]):
            found = found + jnp.where((blocks_ref[k] == index) & (count > k), 1, 0)
        hot.append(found)
    tile = species // 8 * 8
    row = lax.broadcasted_iota(jnp.int32, (rows - tile, lanes), 0) + tile

    def react(columns):
        begin = jnp.concatenate(columns, axis=1)
        operand = begin.astype(BF16)
        begin = operand.astype(F32)
        current = begin
        for _ in range(SECTIONS):
            logits = jnp.dot(logit_w[...], operand, preferred_element_type=F32)
            progress = jnp.exp(logits).astype(BF16)
            both = jnp.dot(gain_w[...], progress, preferred_element_type=F32)
            current = current + both[:rows] / (1.0 + both[rows:])
            operand = current.astype(BF16)
        return (current - begin).astype(BF16).astype(F32)

    for c in first_z:
        c.wait_recv()
    terms = edge_terms(0, packed)
    packed = jnp.zeros((rows, lanes), F32)
    second_x = [x_copies(1, y) for y in range(cells_y)]
    second_y = y_copies(1)
    second_z = z_copies(1)
    done_low, done_high = set(), set()

    def wait_y(stage, copies, y, done):
        for k in range(2):
            for low in (True, False):
                need = y - 2 <= k - 2 if low else y + 2 >= cells_y + k
                if need and (low, k) not in done:
                    done.add((low, k))
                    (y_low if low else y_high)(stage, k).wait_recv()

    for first in range(0, cells_y, GROUP):
        columns, carried, places = [], [], []
        for y in range(first, min(first + GROUP, cells_y)):
            for c in first_x[y]:
                c.wait_recv()
            wait_y(0, first_y, y, done_low)
            for x in range(cells_x):
                v = diffuse(0, x, y, scale, terms)
                heat = jnp.broadcast_to(inverse[x, y : y + 1, :], (rows - tile, lanes))
                last = jnp.where(row < species, v[tile:], 0.0)
                last = jnp.where((row >= species) & (row < species + 2), 1.0, last)
                last = jnp.where((row >= species + 2) & (row < species + 4), heat, last)
                columns.append(jnp.concatenate([v[:tile], last], axis=0))
                carried.append(v)
                places.append((x, y))
        increment = react(columns)
        for k, (x, y) in enumerate(places):
            index = number(x, y)
            is_hot = jnp.broadcast_to(hot[index], (rows, lanes)) > 0
            v = carried[k] + jnp.where(is_hot, increment[:, k * lanes : (k + 1) * lanes], 0.0)
            field[1, y, x] = v
            send[1, y, x] = v.astype(BF16)
            packed = jnp.where(lane // 4 == index, pack(v, index), packed)
        for y in range(first, min(first + GROUP, cells_y)):
            start(second_x[y])
            start(second_y.get(y, []))
    edges_out[1] = packed.astype(BF16)
    start(second_z)

    for c in second_z:
        c.wait_recv()
    terms = edge_terms(1, packed)
    for y in range(cells_y):
        for c in second_x[y]:
            c.wait_recv()
        wait_y(1, second_y, y, done_high)
        for x in range(cells_x):
            v = diffuse(1, x, y, scale, terms)
            out_ref[pl.ds(number(x, y), species, stride=blocks), :] = v[:species]
    for c in waits_send:
        c.wait_send()


def body(
    composition, inv_temp, diffusivity, reactant_orders, net_stoich, log_rate, activation, hot_blocks, hot_counts
):
    species, cells_x, cells_y, lanes = composition.shape
    reactions = reactant_orders.shape[0]
    blocks = cells_x * cells_y
    rows = up(species + 4, 16)
    used = up(reactions, 16)
    tall, broad = up(reactions, 128), up(rows, 128)
    vmem, smem = pl.BlockSpec(memory_space=pltpu.VMEM), pl.BlockSpec(memory_space=pltpu.SMEM)
    out = pl.pallas_call(
        functools.partial(kernel, cells_x, cells_y, species, reactions),
        out_shape=jax.ShapeDtypeStruct((species * blocks, lanes), F32),
        in_specs=[vmem] * 7 + [smem] * 2,
        out_specs=vmem,
        scratch_shapes=[
            pltpu.VMEM((2, cells_y, cells_x, rows, lanes), F32),
            pltpu.VMEM((2, cells_y, cells_x, rows, lanes), BF16),
            pltpu.VMEM((2, rows, lanes), BF16),
            pltpu.VMEM((2, cells_y, 2, rows, lanes), BF16),
            pltpu.VMEM((2, cells_y, 2, rows, lanes), BF16),
            pltpu.VMEM((2, 2, cells_x, rows, lanes), BF16),
            pltpu.VMEM((2, 2, cells_x, rows, lanes), BF16),
            pltpu.VMEM((2, rows, lanes), BF16),
            pltpu.VMEM((2, rows, lanes), BF16),
            pltpu.VMEM((tall, broad), F32),
            pltpu.VMEM((broad, tall), F32),
            pltpu.VMEM((used, rows), BF16),
            pltpu.VMEM((2 * rows, used), BF16),
            pltpu.SemaphoreType.DMA((2, 4 * cells_y)),
            pltpu.SemaphoreType.DMA((2, 8)),
            pltpu.SemaphoreType.DMA((2, 4)),
        ],
        compiler_params=pltpu.CompilerParams(
            collective_id=0, has_side_effects=True, vmem_limit_bytes=32 * 2**20
        ),
        cost_estimate=pl.CostEstimate(
            flops=2 * SECTIONS * 3 * reactions * species * blocks * lanes,
            bytes_accessed=8 * species * blocks * lanes,
            transcendentals=SECTIONS * reactions * blocks * lanes,
        ),
    )(
        composition.reshape(species * blocks, lanes),
        inv_temp,
        diffusivity.reshape(1, species),
        reactant_orders,
        net_stoich,
        log_rate.reshape(1, reactions),
        activation.reshape(1, reactions),
        hot_blocks.reshape(-1),
        hot_counts.reshape(1),
    )
    return out.reshape(composition.shape)


def solution(mesh):
    in_specs = (
        P(None, "gx", "gy", "gz"),
        P("gx", "gy", "gz"),
        P(), P(), P(), P(), P(),
        P("gx", "gy", "gz", None),
        P("gx", "gy", "gz"),
    )
    return jax.shard_map(
        body, mesh=mesh, in_specs=in_specs, out_specs=P(None, "gx", "gy", "gz"), check_vma=False
    )
```

```python
import functools

import jax
import jax.numpy as jnp
from jax import lax
from jax.experimental import pallas as pl
from jax.experimental.pallas import tpu as pltpu
from jax.sharding import PartitionSpec as P

SECTIONS = 4
MESH = pl.DeviceIdType.MESH
F32, BF16 = jnp.float32, jnp.bfloat16
GROUP = 1


def up(value, step):
    return (value + step - 1) // step * step


def kernel(
    cells_x, cells_y, species, reactions,
    comp_hbm, inv_hbm, diff_hbm, orders_hbm, net_hbm, rate_hbm, act_hbm, blocks_hbm, counts_hbm,
    out_ref,
    field, send, edges_out, from_low_x, from_high_x, from_low_y, from_high_y, edges_low, edges_high,
    orders_pad, orders_t, logit_w, gain_w,
    comp, inv_ref, diff_ref, orders_ref, net_ref, rate_ref, act_ref, blocks_ref, counts_ref,
    sems_x, sems_y, sems_z, sems_in,
):
    size_x, size_y, size_z = (lax.axis_size(a) for a in ("gx", "gy", "gz"))
    rows = field.shape[3]
    lanes = field.shape[4]
    blocks = cells_x * cells_y

    def beside(axis, size, step):
        return {axis: lax.rem(lax.axis_index(axis) + (step + size), size)}

    low_x, high_x = beside("gx", size_x, -1), beside("gx", size_x, 1)
    low_y, high_y = beside("gy", size_y, -1), beside("gy", size_y, 1)
    low_z, high_z = beside("gz", size_z, -1), beside("gz", size_z, 1)
    others = [low_x, high_x, low_y, high_y, high_z] + ([low_z] if size_z > 2 else [])

    barrier = pltpu.get_barrier_semaphore()
    for other in others:
        pl.semaphore_signal(barrier, inc=1, device_id=other, device_id_type=MESH)
    loads = [
        pltpu.make_async_copy(src, dst, sems_in.at[k])
        for k, (src, dst) in enumerate((
            (comp_hbm, comp), (orders_hbm, orders_ref), (net_hbm, net_ref), (inv_hbm, inv_ref), (diff_hbm, diff_ref),
            (rate_hbm, rate_ref), (act_hbm, act_ref), (blocks_hbm, blocks_ref), (counts_hbm, counts_ref),
        ))
    ]
    for load in loads:
        load.start()

    lane = lax.broadcasted_iota(jnp.int32, (rows, lanes), 1)
    edge = (lane < 2) | (lane >= lanes - 2)
    place = lane % 4

    def number(x, y):
        return x * cells_y + y

    def copy(src, dst, sems, index, target):
        return pltpu.make_async_remote_copy(
            src_ref=src, dst_ref=dst, send_sem=sems.at[0, index], recv_sem=sems.at[1, index],
            device_id=target, device_id_type=MESH,
        )

    def x_copies(stage, y):
        base = (stage * cells_y + y) * 2
        return [
            copy(send.at[stage, y, pl.ds(cells_x - 2, 2)], from_low_x.at[stage, y], sems_x, base, high_x),
            copy(send.at[stage, y, pl.ds(0, 2)], from_high_x.at[stage, y], sems_x, base + 1, low_x),
        ]

    def y_copies(stage):
        made = {}
        for k in range(2):
            base = (stage * 2 + k) * 2
            made.setdefault(cells_y - 2 + k, []).append(
                copy(send.at[stage, cells_y - 2 + k], from_low_y.at[stage, k], sems_y, base, high_y)
            )
            made.setdefault(k, []).append(
                copy(send.at[stage, k], from_high_y.at[stage, k], sems_y, base + 1, low_y)
            )
        return made

    def y_low(stage, k):
        return copy(send.at[stage, cells_y - 2 + k], from_low_y.at[stage, k], sems_y, (stage * 2 + k) * 2, high_y)

    def y_high(stage, k):
        return copy(send.at[stage, k], from_high_y.at[stage, k], sems_y, (stage * 2 + k) * 2 + 1, low_y)

    def z_copies(stage):
        made = [copy(edges_out.at[stage], edges_low.at[stage], sems_z, stage * 2, high_z)]
        if size_z > 2:
            made.append(copy(edges_out.at[stage], edges_high.at[stage], sems_z, stage * 2 + 1, low_z))
        return made

    def pack(value, index):
        return pltpu.roll(value, (4 * index + 2) % lanes, 1)

    def edge_terms(stage, own):
        low = edges_low[stage].astype(F32)
        got = low if size_z == 2 else jnp.where(place >= 2, edges_high[stage].astype(F32), low)
        d = got - own
        far = jnp.where(place < 2, pltpu.roll(d, lanes - 2, 1), pltpu.roll(d, 2, 1))
        near = jnp.where(place == 1, pltpu.roll(d, lanes - 1, 1), pltpu.roll(d, 1, 1))
        return jnp.where((place == 1) | (place == 2), 16.0 * near, 0.0) - far

    def at_x(stage, x, y):
        if x < 0:
            return from_low_x[stage, y, 2 + x].astype(F32)
        if x >= cells_x:
            return from_high_x[stage, y, x - cells_x].astype(F32)
        return field[stage, y, x]

    def at_y(stage, x, y):
        if y < 0:
            return from_low_y[stage, 2 + y, x].astype(F32)
        if y >= cells_y:
            return from_high_y[stage, y - cells_y, x].astype(F32)
        return field[stage, y, x]

    def diffuse(stage, x, y, scale, terms):
        v = field[stage, y, x]
        near = (
            at_x(stage, x - 1, y) + at_x(stage, x + 1, y) + at_y(stage, x, y - 1) + at_y(stage, x, y + 1)
            + pltpu.roll(v, 1, 1) + pltpu.roll(v, lanes - 1, 1)
        )
        far = (
            at_x(stage, x - 2, y) + at_x(stage, x + 2, y) + at_y(stage, x, y - 2) + at_y(stage, x, y + 2)
            + pltpu.roll(v, 2, 1) + pltpu.roll(v, lanes - 2, 1)
        )
        index = number(x, y)
        fix = jnp.where(edge, pltpu.roll(terms, (2 * lanes - 4 * index - 2) % lanes, 1), 0.0)
        return v + scale * (16.0 * near - far - 90.0 * v + fix)

    waits_send = []

    def start(copies):
        for c in copies:
            c.start()
            waits_send.append(c)

    first_x = [x_copies(0, y) for y in range(cells_y)]
    first_y = y_copies(0)
    first_z = z_copies(0)
    loads[0].wait()
    packed = jnp.zeros((rows, lanes), F32)
    tile = species // 8 * 8
    for y in range(cells_y):
        for x in range(cells_x):
            field[0, y, x, pl.ds(tile, rows - tile), :] = jnp.zeros((rows - tile, lanes), F32)
            field[0, y, x, pl.ds(0, species), :] = comp[pl.ds(number(x, y), species, stride=blocks), :]
            send[0, y, x] = field[0, y, x].astype(BF16)
        if y == 0:
            pl.semaphore_wait(barrier, len(others))
        start(first_x[y])
        start(first_y.get(y, []))
    for y in range(cells_y):
        for x in range(cells_x):
            packed = jnp.where(lane // 4 == number(x, y), pack(field[0, y, x], number(x, y)), packed)
    edges_out[0] = packed.astype(BF16)
    start(first_z)
    for load in loads[1:]:
        load.wait()

    orders_pad[...] = jnp.zeros_like(orders_pad)
    orders_pad[pl.ds(0, reactions), pl.ds(0, species)] = orders_ref[...].astype(F32)
    used = logit_w.shape[0]
    transposed = orders_pad[...].T
    gain_w[pl.ds(rows, rows), :] = (0.5 * transposed[:rows, :used]).astype(BF16)
    orders_t[...] = transposed
    orders_pad[pl.ds(0, reactions), pl.ds(0, species)] = net_ref[...].astype(F32)
    gain_w[pl.ds(0, rows), :] = (0.5 * orders_pad[...].T[:rows, :used]).astype(BF16)
    for k, (ref, sign) in enumerate(((rate_ref, 1.0), (act_ref, -1.0))):
        value = sign * ref[...]
        upper = value.astype(BF16).astype(F32)
        orders_t[pl.ds(species + 2 * k, 1), pl.ds(0, reactions)] = upper
        orders_t[pl.ds(species + 2 * k + 1, 1), pl.ds(0, reactions)] = value - upper
    logit_w[...] = orders_t[...].T[:used, :rows].astype(BF16)
    number_row = diff_ref[...] * (1.0 / 12.0)
    orders_pad[pl.ds(0, lanes), :] = jnp.zeros((lanes, orders_pad.shape[1]), F32)
    orders_pad[pl.ds(0, lanes), pl.ds(0, species)] = jnp.broadcast_to(number_row, (lanes, species))
    scale = orders_pad[pl.ds(0, lanes), :].T[:rows, :]

    inverse = inv_ref[...].astype(F32)
    listed = blocks_ref[...]
    valid = lax.broadcasted_iota(jnp.int32, listed.shape, 1) < counts_ref[0]
    hot = [
        jnp.sum(jnp.where(valid & (listed == index), 1.0, 0.0), axis=1, keepdims=True) for index in range(blocks)
    ]
    row = lax.broadcasted_iota(jnp.int32, (rows - tile, lanes), 0) + tile

    def react(columns):
        begin = jnp.concatenate(columns, axis=1)
        operand = begin.astype(BF16)
        begin = operand.astype(F32)
        current = begin
        for _ in range(SECTIONS):
            logits = jnp.dot(logit_w[...], operand, preferred_element_type=F32)
            progress = jnp.exp(logits).astype(BF16)
            both = jnp.dot(gain_w[...], progress, preferred_element_type=F32)
            current = current + both[:rows] / (1.0 + both[rows:])
            operand = current.astype(BF16)
        return (current - begin).astype(BF16).astype(F32)

    for c in first_z:
        c.wait_recv()
    terms = edge_terms(0, packed)
    packed = jnp.zeros((rows, lanes), F32)
    second_x = [x_copies(1, y) for y in range(cells_y)]
    second_y = y_copies(1)
    second_z = z_copies(1)
    done_low, done_high = set(), set()

    def wait_y(stage, copies, y, done):
        for k in range(2):
            for low in (True, False):
                need = y - 2 <= k - 2 if low else y + 2 >= cells_y + k
                if need and (low, k) not in done:
                    done.add((low, k))
                    (y_low if low else y_high)(stage, k).wait_recv()

    for first in range(0, cells_y, GROUP):
        columns, carried, places = [], [], []
        for y in range(first, min(first + GROUP, cells_y)):
            for c in first_x[y]:
                c.wait_recv()
            wait_y(0, first_y, y, done_low)
            for x in range(cells_x):
                v = diffuse(0, x, y, scale, terms)
                heat = jnp.broadcast_to(inverse[x, y : y + 1, :], (rows - tile, lanes))
                last = jnp.where(row < species, v[tile:], 0.0)
                last = jnp.where((row >= species) & (row < species + 2), 1.0, last)
                last = jnp.where((row >= species + 2) & (row < species + 4), heat, last)
                columns.append(jnp.concatenate([v[:tile], last], axis=0))
                carried.append(v)
                places.append((x, y))
        increment = react(columns)
        for k, (x, y) in enumerate(places):
            index = number(x, y)
            is_hot = jnp.broadcast_to(hot[index], (rows, lanes)) > 0.5
            v = carried[k] + jnp.where(is_hot, increment[:, k * lanes : (k + 1) * lanes], 0.0)
            field[1, y, x] = v
            send[1, y, x] = v.astype(BF16)
            packed = jnp.where(lane // 4 == index, pack(v, index), packed)
        for y in range(first, min(first + GROUP, cells_y)):
            start(second_x[y])
            start(second_y.get(y, []))
    edges_out[1] = packed.astype(BF16)
    start(second_z)

    for c in second_z:
        c.wait_recv()
    terms = edge_terms(1, packed)
    for y in range(cells_y):
        for c in second_x[y]:
            c.wait_recv()
        wait_y(1, second_y, y, done_high)
        for x in range(cells_x):
            v = diffuse(1, x, y, scale, terms)
            out_ref[pl.ds(number(x, y), species, stride=blocks), :] = v[:species]
    for c in waits_send:
        c.wait_send()


def body(
    composition, inv_temp, diffusivity, reactant_orders, net_stoich, log_rate, activation, hot_blocks, hot_counts
):
    species, cells_x, cells_y, lanes = composition.shape
    reactions = reactant_orders.shape[0]
    blocks = cells_x * cells_y
    rows = up(species + 4, 16)
    used = up(reactions, 16)
    tall, broad = up(reactions, 128), up(rows, 128)
    out = pl.pallas_call(
        functools.partial(kernel, cells_x, cells_y, species, reactions),
        out_shape=jax.ShapeDtypeStruct((species * blocks, lanes), F32),
        in_specs=[pl.BlockSpec(memory_space=pltpu.HBM)] * 9,
        out_specs=pl.BlockSpec(memory_space=pltpu.VMEM),
        scratch_shapes=[
            pltpu.VMEM((2, cells_y, cells_x, rows, lanes), F32),
            pltpu.VMEM((2, cells_y, cells_x, rows, lanes), BF16),
            pltpu.VMEM((2, rows, lanes), BF16),
            pltpu.VMEM((2, cells_y, 2, rows, lanes), BF16),
            pltpu.VMEM((2, cells_y, 2, rows, lanes), BF16),
            pltpu.VMEM((2, 2, cells_x, rows, lanes), BF16),
            pltpu.VMEM((2, 2, cells_x, rows, lanes), BF16),
            pltpu.VMEM((2, rows, lanes), BF16),
            pltpu.VMEM((2, rows, lanes), BF16),
            pltpu.VMEM((tall, broad), F32),
            pltpu.VMEM((broad, tall), F32),
            pltpu.VMEM((used, rows), BF16),
            pltpu.VMEM((2 * rows, used), BF16),
            pltpu.VMEM((species * blocks, lanes), F32),
            pltpu.VMEM(inv_temp.shape, BF16),
            pltpu.VMEM((1, species), F32),
            pltpu.VMEM((reactions, species), BF16),
            pltpu.VMEM((reactions, species), BF16),
            pltpu.VMEM((1, reactions), F32),
            pltpu.VMEM((1, reactions), F32),
            pltpu.VMEM((1, hot_blocks.shape[-1]), jnp.int32),
            pltpu.VMEM((1, 1, 1), jnp.int32),
            pltpu.SemaphoreType.DMA((2, 4 * cells_y)),
            pltpu.SemaphoreType.DMA((2, 8)),
            pltpu.SemaphoreType.DMA((2, 4)),
            pltpu.SemaphoreType.DMA((9,)),
        ],
        compiler_params=pltpu.CompilerParams(
            collective_id=0, has_side_effects=True, vmem_limit_bytes=60 * 2**20
        ),
        cost_estimate=pl.CostEstimate(
            flops=2 * SECTIONS * 3 * reactions * species * blocks * lanes,
            bytes_accessed=8 * species * blocks * lanes,
            transcendentals=SECTIONS * reactions * blocks * lanes,
        ),
    )(
        composition.reshape(species * blocks, lanes),
        inv_temp,
        diffusivity.reshape(1, species),
        reactant_orders,
        net_stoich.T,
        log_rate.reshape(1, reactions),
        activation.reshape(1, reactions),
        hot_blocks.reshape(1, -1),
        hot_counts,
    )
    return out.reshape(composition.shape)


def solution(mesh):
    in_specs = (
        P(None, "gx", "gy", "gz"),
        P("gx", "gy", "gz"),
        P(), P(), P(), P(), P(),
        P("gx", "gy", "gz", None),
        P("gx", "gy", "gz"),
    )
    return jax.shard_map(
        body, mesh=mesh, in_specs=in_specs, out_specs=P(None, "gx", "gy", "gz"), check_vma=False
    )
```
